32 devices in a mesh: grp: 4 (over y, x), row: 8 (over z, core).
Axes of the slice: x: 2, y: 2, z: 4, core: 2. Of those that a mesh axis runs over, the one named last changes fastest.
Arguments:
- b_tensor: bfloat16 [9984, 8, 768], P(None, 'grp', 'row'), may hold values from -0.21875 to 0.21875
- aux_counts: int32 [4], replicated, may hold values from 1 to 2, as said below
Outputs:
- exchange_matrix: float32 [9984, 9984], P('row', 'grp')
The draws below stay inside these ranges and needn't reach their ends.
Inputs may be any that keep to these rules, and one draw needn't show every extreme that they name: `aux_counts`: some group has all 2 slots live.
All inputs are finite; a program needn't handle non-finite values.
Results may differ from the reference program's by a relative error of at most 0.0003.
Values may be sent and summed in bfloat16 or wider, within the bound.
A program may use at most 256 MiB of HBM per device.

```python
import jax
import jax.numpy as jnp
from jax import lax

NBF = 9984
NOCC = 768
APG = 2
SLOTS = 8
N_GRP = 4


def draw_aux_counts(key, part):
    counts = jax.random.randint(key, (N_GRP,), 1, APG + 1)
    chosen = jax.random.randint(jax.random.fold_in(key, 7), (), 0, N_GRP)
    return counts.at[chosen].set(APG).astype(jnp.int32)


def steps_of(own_key, shape, cuts, least, largest):
    def one(axis_at, shards_of):
        steps = jax.random.uniform(jax.random.fold_in(jax.random.fold_in(own_key, 6), axis_at), (shards_of,), jnp.float32, least / len(cuts), largest / len(cuts))
        return jnp.repeat(jnp.exp(steps), shape[axis_at] // shards_of).reshape((-1,) + (1,) * (len(shape) - axis_at - 1))

    gain = one(*cuts[0])
    for cut in cuts[1:]:
        gain = gain * one(*cut)
    return gain


def normal_values(stream_key, shape, width, bound, split=(), kind=jnp.bfloat16):
    values = width * jax.random.normal(stream_key, shape, jnp.float32)
    if split:
        values = values * steps_of(stream_key, shape, split, -0.22, 0.18)
    return jnp.clip(values, -bound, bound).astype(kind)


def setup_inputs(seed: int = 0) -> dict:
    seeds = jax.random.split(jax.random.key(seed), 3)
    return {
        "b_tensor": normal_values(seeds[0], (NBF, SLOTS, NOCC), NOCC ** -0.5, 0.21875, ((1, 4), (2, 8))),
        "aux_counts": draw_aux_counts(jax.random.fold_in(seeds[2], 71), 0),
    }


def reference(b_tensor, aux_counts):
    slot_index = jnp.arange(SLOTS)
    group_of = slot_index // APG
    live_mask = (slot_index % APG) < aux_counts[group_of]
    masked = b_tensor * live_mask.astype(jnp.bfloat16)[None, :, None]
    stacked = masked.reshape(NBF, SLOTS * NOCC).astype(jnp.float32)
    return jnp.dot(stacked, stacked.T, precision=lax.Precision.HIGHEST, preferred_element_type=jnp.float32)
```

```python
import jax
import jax.numpy as jnp
from jax import lax
from jax.experimental import pallas as pl
from jax.experimental.layout import Layout, with_layout_constraint
from jax.experimental.pallas import tpu as pltpu
from jax.sharding import PartitionSpec as P

LAG = 4


def masked_depth(b_tensor, aux_counts):
    group_index = lax.axis_index("grp")
    slot_count = b_tensor.shape[1]
    live_count = lax.dynamic_index_in_dim(aux_counts, group_index, 0, keepdims=False)
    live_mask = (jnp.arange(slot_count) < live_count).astype(jnp.bfloat16)
    return (b_tensor * live_mask[None, :, None]).reshape(b_tensor.shape[0], -1)


def product(rows, cols):
    return lax.dot_general(
        rows, cols, (((1,), (1,)), ((), ())), preferred_element_type=jnp.float32
    )


def general_shards(b_tensor, aux_counts):
    masked = masked_depth(b_tensor, aux_counts)
    depth = masked.shape[1]
    cols = lax.all_to_all(masked, "grp", split_axis=0, concat_axis=1, tiled=True)
    cols = lax.all_gather(cols, "row", axis=1, tiled=True)
    rows = lax.all_to_all(masked, "row", split_axis=0, concat_axis=1, tiled=True)
    rows = rows.reshape(rows.shape[0], -1, depth)
    rows = lax.all_gather(rows, "grp", axis=2, tiled=True)
    return product(rows.reshape(rows.shape[0], -1), cols)


def gather_kernel(own, cols, rows, own_sem, a_send, u_recv, right_send, left_send,
                  core_send, core_recv, hop_send, hop_recv):
    groups, block, depth = own.shape
    g = lax.axis_index("grp")
    r = lax.axis_index("row")
    z, c = r // 2, r % 2
    gy, gx = g // 2, g % 2
    sy, sx = z // 2, z % 2
    side_y, side_x = (gy + sy) % 2, (gx + sx) % 2
    partner = z * 2 + 1 - c

    def flipped(y, x, m):
        return (y + m // 2) % 2 * 2 + (x + m) % 2

    def at(chunk):
        return pl.ds(pl.multiple_of(chunk * depth, depth), depth)

    mine = pl.ds(pl.multiple_of(c * block, block), block)
    theirs = pl.ds(pl.multiple_of((1 - c) * block, block), block)

    def remote(src, dst, send, recv, grp, row):
        return pltpu.make_async_remote_copy(
            src_ref=src, dst_ref=dst, send_sem=send, recv_sem=recv,
            device_id={"grp": grp, "row": row}, device_id_type=pl.DeviceIdType.MESH)

    barrier = pltpu.get_barrier_semaphore()

    def greet(grp, row):
        pl.semaphore_signal(barrier, inc=1, device_id={"grp": grp, "row": row},
                            device_id_type=pl.DeviceIdType.MESH)

    greet(g, partner)
    for m in range(1, groups):
        greet(flipped(gy, gx, m), r)

    @pl.when(z > 0)
    def _():
        greet(g, r - 2)

    @pl.when(z < groups - 1)
    def _():
        greet(g, r + 2)

    inner = (z > 0).astype(jnp.int32) + (z < groups - 1).astype(jnp.int32)
    pl.semaphore_wait(barrier, groups + inner)

    here = z * groups + g

    def to_group(m):
        peer = flipped(gy, gx, m)
        return remote(own.at[peer], cols.at[mine, at(here)], a_send.at[m],
                      u_recv.at[here], peer, r)

    keep_own = pltpu.make_async_copy(own.at[g], cols.at[mine, at(here)], own_sem)
    keep_own.start()
    for m in range(1, groups):
        to_group(m).start()

    def right(q):
        return remote(cols.at[mine, at(q)], cols.at[mine, at(q)], right_send.at[q],
                      u_recv.at[q], g, r + 2)

    def left(q):
        return remote(cols.at[mine, at(q)], cols.at[mine, at(q)], left_send.at[q],
                      u_recv.at[q], g, r - 2)

    def core(q):
        return remote(cols.at[mine, at(q)], cols.at[mine, at(q)], core_send.at[q],
                      core_recv.at[q], g, partner)

    def hop(src, q, m):
        return remote(src, rows.at[:, at(q)], hop_send.at[q], hop_recv.at[q],
                      flipped(gy, gx, m), r)

    is_source = side_y + side_x == 0

    def step_of(t):
        k, m, side = t // 8, t % 8 // 2, t % 2
        zs = z + (2 * side - 1) * k
        valid = ((k > 0) | (side == 0)) & (zs >= 0) & (zs < groups)
        return k, m, zs, valid

    def hop_mask(m):
        odd = m % 2
        near = (1 - odd) * side_x + odd * side_y
        far = (1 - odd) * side_y + odd * side_x
        last = (near == 0) & (far == 1)
        first_mask = 1 + odd
        second_mask = 2 - odd
        turn = near * (1 - far)
        return turn * second_mask + (1 - turn) * first_mask, last

    steps = groups * groups * 2

    def pass_on(late, place):
        k, m, zs, valid = step_of(jnp.maximum(late, 0))
        mask, last = hop_mask(m)
        near = (1 - m % 2) * side_x + m % 2 * side_y
        here_now = (near == 1) & (side_x + side_y == place)

        @pl.when((late >= 0) & valid & here_now)
        def _():
            q = zs * groups + flipped(sy, sx, m)
            forward = hop(rows.at[:, at(q)], q, mask)
            forward.wait_recv()
            forward.start()

    def advance(t, carry):
        k, m, zs, valid = step_of(t)

        @pl.when((t < steps) & valid)
        def _():
            q = zs * groups + flipped(gy, gx, m)
            is_own = (k == 0) & (m == 0)

            @pl.when(is_own)
            def _():
                keep_own.wait()

            @pl.when(jnp.logical_not(is_own))
            def _():
                core_like = remote(cols.at[mine, at(q)], cols.at[mine, at(q)],
                                   core_send.at[q], u_recv.at[q], g, partner)
                core_like.wait_recv()

            @pl.when((zs <= z) & (z < groups - 1))
            def _():
                right(q).start()

            @pl.when((zs >= z) & (z > 0))
            def _():
                left(q).start()

            core(q).start()

            @pl.when(is_source)
            def _():
                hop(cols.at[mine, at(q)], q, hop_mask(m)[0]).start()

        for place in (1, 2):
            pass_on(t - LAG * place, place)

        return carry

    lax.fori_loop(0, steps + 2 * LAG, advance, 0)

    for m in range(1, groups):
        to_group(m).wait_send()

    def drain(q, carry):
        zs, gs = q // groups, q % groups

        @pl.when((zs <= z) & (z < groups - 1))
        def _():
            right(q).wait_send()

        @pl.when((zs >= z) & (z > 0))
        def _():
            left(q).wait_send()

        core(q).wait_send()
        remote(cols.at[theirs, at(q)], cols.at[theirs, at(q)], core_send.at[q],
               core_recv.at[q], g, partner).wait_recv()
        odd = (gs % 2 + sx) % 2
        mask, last = hop_mask(odd)

        @pl.when(jnp.logical_not(last))
        def _():
            hop(rows.at[:, at(q)], q, mask).wait_send()

        @pl.when(last)
        def _():
            hop(rows.at[:, at(q)], q, mask).wait_recv()

        return carry

    lax.fori_loop(0, groups * groups, drain, 0)


def square_shards(b_tensor, aux_counts):
    groups = lax.axis_size("grp")
    row_count = lax.axis_size("row")
    masked = masked_depth(b_tensor, aux_counts)
    masked = with_layout_constraint(masked, Layout(major_to_minor=(0, 1)))
    depth = masked.shape[1]
    c = lax.axis_index("row") % 2
    halves = masked.reshape(groups, 2, -1, depth)
    mine = lax.dynamic_index_in_dim(halves, c, 1, keepdims=False)
    other = lax.dynamic_index_in_dim(halves, 1 - c, 1, keepdims=False)
    swap = [(i, i + 1 - 2 * (i % 2)) for i in range(row_count)]
    got = lax.ppermute(other, "row", swap)
    own = jnp.concatenate(
        [jnp.where(c == 0, mine, got), jnp.where(c == 0, got, mine)], axis=2
    )
    block = own.shape[1]
    chunks = groups * groups
    dma = pltpu.SemaphoreType.DMA
    anywhere = pl.BlockSpec(memory_space=pl.ANY)
    cols, rows = pl.pallas_call(
        gather_kernel,
        out_shape=[
            jax.ShapeDtypeStruct((2 * block, chunks * 2 * depth), jnp.bfloat16),
            jax.ShapeDtypeStruct((block, chunks * 2 * depth), jnp.bfloat16),
        ],
        in_specs=[anywhere],
        out_specs=[anywhere, anywhere],
        scratch_shapes=[dma, dma((groups,))] + [dma((chunks,))] * 7,
        compiler_params=pltpu.CompilerParams(collective_id=0, has_side_effects=True),
    )(own)
    place = jnp.where(lax.axis_index("row") // 2 == lax.axis_index("grp"), 1 + c, 0)
    return lax.switch(
        place,
        [
            lambda rows, cols: product(rows, cols),
            lambda rows, cols: product(cols[:block], cols),
            lambda rows, cols: product(cols[block:], cols),
        ],
        rows,
        cols,
    )


def solution(mesh):
    groups, row_count = mesh.shape["grp"], mesh.shape["row"]
    square = groups == 4 and row_count == 2 * groups
    return jax.shard_map(
        square_shards if square else general_shards,
        mesh=mesh,
        in_specs=(P(None, "grp", "row"), P()),
        out_specs=P("row", "grp"),
        check_vma=False,
    )
```

```python
import jax
import jax.numpy as jnp
from jax import lax
from jax.experimental import pallas as pl
from jax.experimental.layout import Layout, with_layout_constraint
from jax.experimental.pallas import tpu as pltpu
from jax.sharding import PartitionSpec as P

LAG = 4


def masked_depth(b_tensor, aux_counts):
    group_index = lax.axis_index("grp")
    slot_count = b_tensor.shape[1]
    live_count = lax.dynamic_index_in_dim(aux_counts, group_index, 0, keepdims=False)
    live_mask = (jnp.arange(slot_count) < live_count).astype(jnp.bfloat16)
    return (b_tensor * live_mask[None, :, None]).reshape(b_tensor.shape[0], -1)


def product(rows, cols):
    return lax.dot_general(
        rows, cols, (((1,), (1,)), ((), ())), preferred_element_type=jnp.float32
    )


def general_shards(b_tensor, aux_counts):
    masked = masked_depth(b_tensor, aux_counts)
    depth = masked.shape[1]
    cols = lax.all_to_all(masked, "grp", split_axis=0, concat_axis=1, tiled=True)
    cols = lax.all_gather(cols, "row", axis=1, tiled=True)
    rows = lax.all_to_all(masked, "row", split_axis=0, concat_axis=1, tiled=True)
    rows = rows.reshape(rows.shape[0], -1, depth)
    rows = lax.all_gather(rows, "grp", axis=2, tiled=True)
    return product(rows.reshape(rows.shape[0], -1), cols)


def gather_kernel(own, cols, rows, own_sem, a_send, u_recv, right_send, left_send,
                  core_send, core_recv, hop_send, hop_recv):
    groups, block, depth = own.shape
    g = lax.axis_index("grp")
    r = lax.axis_index("row")
    z, c = r // 2, r % 2
    gy, gx = g // 2, g % 2
    sy, sx = z // 2, z % 2
    side_y, side_x = (gy + sy) % 2, (gx + sx) % 2
    partner = z * 2 + 1 - c

    def flipped(y, x, m):
        return (y + m // 2) % 2 * 2 + (x + m) % 2

    def at(chunk):
        return pl.ds(pl.multiple_of(chunk * depth, depth), depth)

    mine = pl.ds(pl.multiple_of(c * block, block), block)
    theirs = pl.ds(pl.multiple_of((1 - c) * block, block), block)

    def remote(src, dst, send, recv, grp, row):
        return pltpu.make_async_remote_copy(
            src_ref=src, dst_ref=dst, send_sem=send, recv_sem=recv,
            device_id={"grp": grp, "row": row}, device_id_type=pl.DeviceIdType.MESH)

    barrier = pltpu.get_barrier_semaphore()

    def greet(grp, row):
        pl.semaphore_signal(barrier, inc=1, device_id={"grp": grp, "row": row},
                            device_id_type=pl.DeviceIdType.MESH)

    greet(g, partner)
    for m in range(1, groups):
        greet(flipped(gy, gx, m), r)

    @pl.when(z > 0)
    def _():
        greet(g, r - 2)

    @pl.when(z < groups - 1)
    def _():
        greet(g, r + 2)

    inner = (z > 0).astype(jnp.int32) + (z < groups - 1).astype(jnp.int32)
    pl.semaphore_wait(barrier, groups + inner)

    here = z * groups + g

    def to_group(m):
        peer = flipped(gy, gx, m)
        return remote(own.at[peer], cols.at[mine, at(here)], a_send.at[m],
                      u_recv.at[here], peer, r)

    keep_own = pltpu.make_async_copy(own.at[g], cols.at[mine, at(here)], own_sem)
    keep_own.start()
    for m in range(1, groups):
        to_group(m).start()

    def right(q, src=None):
        src = cols.at[mine, at(q)] if src is None else src
        return remote(src, cols.at[mine, at(q)], right_send.at[q],
                      u_recv.at[q], g, r + 2)

    def left(q, src=None):
        src = cols.at[mine, at(q)] if src is None else src
        return remote(src, cols.at[mine, at(q)], left_send.at[q],
                      u_recv.at[q], g, r - 2)

    def core(q, src=None):
        src = cols.at[mine, at(q)] if src is None else src
        return remote(src, cols.at[mine, at(q)], core_send.at[q],
                      core_recv.at[q], g, partner)

    def hop(src, q, m):
        return remote(src, rows.at[:, at(q)], hop_send.at[q], hop_recv.at[q],
                      flipped(gy, gx, m), r)

    is_source = side_y + side_x == 0

    def step_of(t):
        k, m, side = t // 8, t % 8 // 2, t % 2
        zs = z + (2 * side - 1) * k
        valid = ((k > 0) | (side == 0)) & (zs >= 0) & (zs < groups)
        return k, m, zs, valid

    def hop_mask(m):
        odd = m % 2
        near = (1 - odd) * side_x + odd * side_y
        far = (1 - odd) * side_y + odd * side_x
        last = (near == 0) & (far == 1)
        first_mask = 1 + odd
        second_mask = 2 - odd
        turn = near * (1 - far)
        return turn * second_mask + (1 - turn) * first_mask, last

    steps = groups * groups * 2

    def pass_on(late, place):
        k, m, zs, valid = step_of(jnp.maximum(late, 0))
        mask, last = hop_mask(m)
        near = (1 - m % 2) * side_x + m % 2 * side_y
        here_now = (near == 1) & (side_x + side_y == place)

        @pl.when((late >= 0) & valid & here_now)
        def _():
            q = zs * groups + flipped(sy, sx, m)
            forward = hop(rows.at[:, at(q)], q, mask)
            forward.wait_recv()
            forward.start()

    def send_on(src, q, zs, m):
        @pl.when((zs <= z) & (z < groups - 1))
        def _():
            right(q, src).start()

        @pl.when((zs >= z) & (z > 0))
        def _():
            left(q, src).start()

        core(q, src).start()

        @pl.when(is_source)
        def _():
            hop(src, q, hop_mask(m)[0]).start()

    def advance(t, carry):
        k, m, zs, valid = step_of(t)

        @pl.when((t < steps) & valid)
        def _():
            q = zs * groups + flipped(gy, gx, m)
            is_own = (k == 0) & (m == 0)

            @pl.when(is_own)
            def _():
                send_on(own.at[g], q, zs, m)

            @pl.when(jnp.logical_not(is_own))
            def _():
                held = cols.at[mine, at(q)]
                remote(held, held, core_send.at[q], u_recv.at[q], g, partner).wait_recv()
                send_on(held, q, zs, m)

        for place in (1, 2):
            pass_on(t - LAG * place, place)

        return carry

    lax.fori_loop(0, steps + 2 * LAG, advance, 0)

    for m in range(1, groups):
        to_group(m).wait_send()

    keep_own.wait()

    def drain(q, carry):
        zs, gs = q // groups, q % groups

        @pl.when((zs <= z) & (z < groups - 1))
        def _():
            right(q).wait_send()

        @pl.when((zs >= z) & (z > 0))
        def _():
            left(q).wait_send()

        core(q).wait_send()
        remote(cols.at[theirs, at(q)], cols.at[theirs, at(q)], core_send.at[q],
               core_recv.at[q], g, partner).wait_recv()
        odd = (gs % 2 + sx) % 2
        mask, last = hop_mask(odd)

        @pl.when(jnp.logical_not(last))
        def _():
            hop(rows.at[:, at(q)], q, mask).wait_send()

        @pl.when(last)
        def _():
            hop(rows.at[:, at(q)], q, mask).wait_recv()

        return carry

    lax.fori_loop(0, groups * groups, drain, 0)


def square_shards(b_tensor, aux_counts):
    groups = lax.axis_size("grp")
    row_count = lax.axis_size("row")
    masked = masked_depth(b_tensor, aux_counts)
    masked = with_layout_constraint(masked, Layout(major_to_minor=(0, 1)))
    depth = masked.shape[1]
    c = lax.axis_index("row") % 2
    halves = masked.reshape(groups, 2, -1, depth)
    mine = lax.dynamic_index_in_dim(halves, c, 1, keepdims=False)
    other = lax.dynamic_index_in_dim(halves, 1 - c, 1, keepdims=False)
    swap = [(i, i + 1 - 2 * (i % 2)) for i in range(row_count)]
    got = lax.ppermute(other, "row", swap)
    own = jnp.concatenate(
        [jnp.where(c == 0, mine, got), jnp.where(c == 0, got, mine)], axis=2
    )
    block = own.shape[1]
    chunks = groups * groups
    dma = pltpu.SemaphoreType.DMA
    anywhere = pl.BlockSpec(memory_space=pl.ANY)
    cols, rows = pl.pallas_call(
        gather_kernel,
        out_shape=[
            jax.ShapeDtypeStruct((2 * block, chunks * 2 * depth), jnp.bfloat16),
            jax.ShapeDtypeStruct((block, chunks * 2 * depth), jnp.bfloat16),
        ],
        in_specs=[anywhere],
        out_specs=[anywhere, anywhere],
        scratch_shapes=[dma, dma((groups,))] + [dma((chunks,))] * 7,
        compiler_params=pltpu.CompilerParams(collective_id=0, has_side_effects=True),
    )(own)
    place = jnp.where(lax.axis_index("row") // 2 == lax.axis_index("grp"), 1 + c, 0)
    return lax.switch(
        place,
        [
            lambda rows, cols: product(rows, cols),
            lambda rows, cols: product(cols[:block], cols),
            lambda rows, cols: product(cols[block:], cols),
        ],
        rows,
        cols,
    )


def solution(mesh):
    groups, row_count = mesh.shape["grp"], mesh.shape["row"]
    square = groups == 4 and row_count == 2 * groups
    return jax.shard_map(
        square_shards if square else general_shards,
        mesh=mesh,
        in_specs=(P(None, "grp", "row"), P()),
        out_specs=P("row", "grp"),
        check_vma=False,
    )
```
